128 devices in a mesh: samp: 16 (over x_hi, z, core), par: 8 (over x_lo, y).
Axes of the slice: x: 4 (x_hi: 2, x_lo: 2; x = x_hi * 2 + x_lo), y: 4, z: 4, core: 2. Of those that a mesh axis runs over, the one named last changes fastest.
Arguments:
- jacobian: bfloat16 [65536, 16384], P(('samp', 'par')), may hold values from -6 to 6
- energy: float32 [65536], P('samp'), may hold values from -6 to 6
Outputs:
- update: float32 [16384], P('par')
- residual: float32 [16384], P('par')
The draws below stay inside these ranges and needn't reach their ends.
All inputs are finite; a program needn't handle non-finite values.
Results may differ from the reference program's by a relative error of at most 0.033.
Values may be sent and summed in bfloat16 or wider, within the bound.
A program may use at most 128 MiB of HBM per device.

```python
import jax
import jax.numpy as jnp

PARAMS = 16384
ITERS = 3
SAMPLES = 65536


def draw_jacobian(key, part):
    key = jax.random.fold_in(key, 11)
    first = jax.random.fold_in(key, 0)
    return jax.random.truncated_normal(first, -6.0, 6.0, (SAMPLES, PARAMS), jnp.float32).astype(jnp.bfloat16)


def shard_levels(rng, shape, pieces, smallest, largest):
    def one(dim, blocks):
        steps = jax.random.uniform(jax.random.fold_in(jax.random.fold_in(rng, 6), dim), (blocks,), jnp.float32, smallest / len(pieces), largest / len(pieces))
        return jnp.repeat(jnp.exp(steps), shape[dim] // blocks).reshape((-1,) + (1,) * (len(shape) - dim - 1))

    loudness = one(*pieces[0])
    for cut in pieces[1:]:
        loudness = loudness * one(*cut)
    return loudness


def normal_values(own_key, shape, scale, reach, shards=(), dtype=jnp.bfloat16):
    values = scale * jax.random.normal(own_key, shape, jnp.float32)
    if shards:
        values = values * shard_levels(own_key, shape, shards, -0.22, 0.18)
    return jnp.clip(values, -reach, reach).astype(dtype)


def setup_inputs(seed: int = 0) -> dict:
    key_list = jax.random.split(jax.random.key(seed), 3)
    return {
        "jacobian": draw_jacobian(jax.random.fold_in(key_list[2], 71), 0),
        "energy": normal_values(key_list[1], (SAMPLES,), 1.0, 6.0, ((0, 16),), jnp.float32),
    }


damping = 0.05


def reference(jacobian, energy):
    total = jacobian.shape[0]
    deviation = energy.astype(jnp.bfloat16)
    force = jnp.dot(deviation, jacobian, preferred_element_type=jnp.float32) / total

    def operate(vector):
        narrow = vector.astype(jnp.bfloat16)
        inner = jnp.dot(jacobian, narrow, preferred_element_type=jnp.float32).astype(jnp.bfloat16)
        return jnp.dot(inner, jacobian, preferred_element_type=jnp.float32) / total + damping * vector

    update = jnp.zeros_like(force)
    residual = force
    direction = force
    norm_now = jnp.sum(residual * residual)
    for step in range(ITERS):
        image = operate(direction)
        alpha = norm_now / jnp.sum(direction * image)
        update = update + alpha * direction
        residual = residual - alpha * image
        norm_next = jnp.sum(residual * residual)
        direction = residual + (norm_next / norm_now) * direction
        norm_now = norm_next
    return update, residual
```

```python
import functools

import jax
import jax.numpy as jnp
from jax import lax
from jax.experimental import pallas as pl
from jax.experimental.pallas import tpu as pltpu
from jax.sharding import PartitionSpec as P

ITERS = 3
DAMPING = 0.05
LANES = 128
CHUNKS = 4
MESH = pl.DeviceIdType.MESH
f32, bf16 = jnp.float32, jnp.bfloat16


def coordinates():
    samp, par = lax.axis_index("samp"), lax.axis_index("par")
    x = (samp // 8) * 2 + par // 4
    return x, par % 4, (samp // 2) % 4, samp % 2


def device(x, y, z, c):
    return ((x // 2) * 8 + z * 2 + c, (x % 2) * 4 + y)


def kernel(
    total,
    energy, jac_hbm, update_out, residual_out,
    jac, part, core_out, core_in, plane, axis,
    update, residual, direction, image, wide, narrow,
    load_sem, core_send, core_recv, plane_send, plane_recv, axis_send, axis_recv,
):
    rows, params = jac.shape
    width = params // CHUNKS
    tall = width // LANES
    half = tall // 2
    x, y, z, c = coordinates()
    me = x * 4 + y
    own = c * 4 + z
    sibling = device(x, y, z, 1 - c)
    plane_peers = [
        device((x + a) % 4, (y + b) % 4, z, c) for a in range(4) for b in range(4) if a or b
    ]
    axis_peers = [device(x, y, (z + d) % 4, c) for d in (1, 2, 3)]
    axis_peers += [device(x, y, (z + d) % 4, 1 - c) for d in (1, 2, 3, 0)]

    def load(k):
        columns = pl.ds(k * width, width)
        return pltpu.make_async_copy(jac_hbm.at[:, columns], jac.at[:, columns], load_sem.at[k])

    for k in range(CHUNKS):
        load(k).start()

    barrier = pltpu.get_barrier_semaphore()
    for peer in plane_peers + axis_peers:
        pl.semaphore_signal(barrier, inc=1, device_id=peer, device_id_type=MESH)
    pl.semaphore_wait(barrier, len(plane_peers) + len(axis_peers))

    def core_copy(p, k):
        return pltpu.make_async_remote_copy(
            core_out.at[p, k], core_in.at[p, k], core_send.at[p, k], core_recv.at[p, k],
            device_id=sibling, device_id_type=MESH,
        )

    def slot_copy(buffer, send, recv, p, k, slot, peer):
        return pltpu.make_async_remote_copy(
            buffer.at[p, k, slot], buffer.at[p, k, slot], send.at[p, k], recv.at[p, k],
            device_id=peer, device_id_type=MESH,
        )

    plane_copy = functools.partial(slot_copy, plane, plane_send, plane_recv)
    axis_copy = functools.partial(slot_copy, axis, axis_send, axis_recv)
    plane_all, axis_all = pl.ds(0, len(plane_peers)), pl.ds(0, len(axis_peers))

    def to_plane(p, k):
        core_copy(p, k).wait_recv()
        mine = part[pl.ds(k * tall + c * half, half)] + core_in[p, k].astype(f32)
        plane[p, k, me] = mine.astype(bf16)
        for peer in plane_peers:
            plane_copy(p, k, me, peer).start()

    def to_axis(p, k):
        plane_copy(p, k, plane_all, sibling).wait_recv()
        mine = jnp.sum(plane[p, k].astype(f32), axis=0)
        axis[p, k, own] = mine.astype(bf16)
        for peer in axis_peers:
            axis_copy(p, k, own, peer).start()

    def send_out(p, vector, first):
        for k in range(CHUNKS):
            if first:
                load(k).wait()
            product = jnp.dot(vector, jac[:, k * width : (k + 1) * width], preferred_element_type=f32)
            for i in range(tall):
                part[k * tall + i : k * tall + i + 1] = product[:1, i * LANES : (i + 1) * LANES]
            core_out[p, k] = part[pl.ds(k * tall + (1 - c) * half, half)].astype(bf16)
            core_copy(p, k).start()
            if k >= 1:
                to_plane(p, k - 1)
        to_plane(p, CHUNKS - 1)
        for k in range(CHUNKS):
            to_axis(p, k)

    def arrive(p, k):
        axis_copy(p, k, axis_all, sibling).wait_recv()
        for h in range(2):
            value = jnp.sum(axis[p, k, h * 4 : h * 4 + 4].astype(f32), axis=0)
            image[k * tall + h * half : k * tall + (h + 1) * half] = value * (1.0 / total)

    def forward(k):
        value = image[k * tall : (k + 1) * tall]
        high = value.astype(bf16).astype(f32)
        wide[0] = high
        wide[1] = value - high
        for i in range(tall):
            columns = slice(i * LANES, (i + 1) * LANES)
            narrow[0:1, columns] = wide[0, i : i + 1]
            narrow[1:2, columns] = wide[1, i : i + 1]
        out = lax.dot_general(
            narrow[...].astype(bf16), jac[:, k * width : (k + 1) * width],
            (((1,), (1,)), ((), ())), preferred_element_type=f32,
        )
        return out[0:1] + out[1:2]

    def drain(p):
        for k in range(CHUNKS):
            core_copy(p, k).wait_send()
            plane_copy(p, k, plane_all, sibling).wait_send()
            axis_copy(p, k, axis_all, sibling).wait_send()

    def row8(row):
        return jnp.broadcast_to(row, (8, rows)).astype(bf16)

    def scalar(value):
        return jnp.sum(value, keepdims=True)

    narrow[...] = jnp.zeros(narrow.shape, f32)
    start = lax.axis_index("par") * (rows // LANES)
    deviation = jnp.concatenate(
        [energy[pl.ds(start + i, 1), :] for i in range(rows // LANES)], axis=1
    )
    send_out(0, row8(deviation), True)
    inner = jnp.zeros((1, rows), f32)
    for k in range(CHUNKS):
        arrive(0, k)
        inner += forward(k)
    drain(0)
    force = image[...]
    residual[...] = force
    direction[...] = force
    update[...] = jnp.zeros(force.shape, f32)
    norm = scalar(force * force)

    def advance(norm):
        image[...] = image[...] + DAMPING * direction[...]
        alpha = norm / scalar(direction[...] * image[...])
        update[...] = update[...] + alpha * direction[...]
        residual[...] = residual[...] - alpha * image[...]
        return alpha

    def step(it, carry):
        norm, left, along = carry
        p = (it + 1) % 2
        send_out(p, row8(along), False)
        inner = DAMPING * along
        for k in range(CHUNKS):
            arrive(p, k)
            inner += forward(k)
        drain(p)
        alpha = advance(norm)
        new = scalar(residual[...] * residual[...])
        beta = new / norm
        direction[...] = residual[...] + beta * direction[...]
        left = left - alpha * inner
        return new, left, left + beta * along

    norm, left, along = lax.fori_loop(0, ITERS - 1, step, (norm, inner, inner))
    p = ITERS % 2
    send_out(p, row8(along), False)
    for k in range(CHUNKS):
        arrive(p, k)
    drain(p)
    advance(norm)
    mine = pl.ds(lax.axis_index("par") * update_out.shape[0], update_out.shape[0])
    update_out[...] = update[mine]
    residual_out[...] = residual[mine]


def body(jacobian, energy):
    rows, params = jacobian.shape
    total = rows * lax.axis_size("samp") * lax.axis_size("par")
    tall = params // CHUNKS // LANES
    whole = (params // LANES, LANES)
    piece = (tall // 2, LANES)
    out = jax.ShapeDtypeStruct((params // lax.axis_size("par") // LANES, LANES), f32)
    vmem = pl.BlockSpec(memory_space=pltpu.VMEM)
    dma = pltpu.SemaphoreType.DMA
    update, residual = pl.pallas_call(
        functools.partial(kernel, total),
        out_shape=(out, out),
        in_specs=[vmem, pl.BlockSpec(memory_space=pl.ANY)],
        out_specs=(vmem, vmem),
        scratch_shapes=[
            pltpu.VMEM((rows, params), bf16),
            pltpu.VMEM(whole, f32),
            pltpu.VMEM((2, CHUNKS, *piece), bf16),
            pltpu.VMEM((2, CHUNKS, *piece), bf16),
            pltpu.VMEM((2, CHUNKS, 16, *piece), bf16),
            pltpu.VMEM((2, CHUNKS, 8, *piece), bf16),
            pltpu.VMEM(whole, f32),
            pltpu.VMEM(whole, f32),
            pltpu.VMEM(whole, f32),
            pltpu.VMEM(whole, f32),
            pltpu.VMEM((2, tall, LANES), f32),
            pltpu.VMEM((8, params // CHUNKS), f32),
            dma((CHUNKS,)),
        ]
        + [dma((2, CHUNKS))] * 6,
        compiler_params=pltpu.CompilerParams(
            collective_id=0, has_side_effects=True, vmem_limit_bytes=56 * 2**20
        ),
    )(energy.reshape(-1, LANES), jacobian)
    return update.reshape(-1), residual.reshape(-1)


def solution(mesh):
    return jax.shard_map(
        body,
        mesh=mesh,
        in_specs=(P(("samp", "par"), None), P("samp")),
        out_specs=(P("par"), P("par")),
        check_vma=False,
    )
```

```python
import functools

import jax
import jax.numpy as jnp
from jax import lax
from jax.experimental import pallas as pl
from jax.experimental.pallas import tpu as pltpu
from jax.sharding import PartitionSpec as P

ITERS = 3
DAMPING = 0.05
LANES = 128
CHUNKS = 4
VECTOR_TILES = 12
MESH = pl.DeviceIdType.MESH
f32, bf16 = jnp.float32, jnp.bfloat16


def coordinates():
    samp, par = lax.axis_index("samp"), lax.axis_index("par")
    x = (samp // 8) * 2 + par // 4
    return x, par % 4, (samp // 2) % 4, samp % 2


def device(x, y, z, c):
    return ((x // 2) * 8 + z * 2 + c, (x % 2) * 4 + y)


def hops(*steps):
    return -sum(min(s, 4 - s) for s in steps)


def kernel(
    total,
    energy, jac_hbm, outs,
    jac, jac_t, part, spread, column_out, column, plane, last_out, last, scalar_column, scalar_plane,
    update, residual, direction, image, wide, narrow,
    load_sem, column_send, column_recv, plane_send, plane_recv, core_send, core_recv,
    last_send, last_recv, scalar_send, scalar_recv,
):
    rows, params = jac.shape
    width = params // CHUNKS
    tall = width // LANES
    half = tall // 2
    x, y, z, c = coordinates()
    me = x * 4 + y
    own = c * 4 + z
    sibling = device(x, y, z, 1 - c)
    plane_peers = [
        device((x + a) % 4, (y + b) % 4, z, c)
        for a, b in sorted(((a, b) for a in range(4) for b in range(4) if a or b), key=lambda s: hops(*s))
    ]
    column_peers = [
        ((c + e) % 2, device(x, y, (z + d) % 4, (c + e) % 2))
        for d, e in sorted(((d, e) for d in range(4) for e in range(2) if d or e), key=lambda s: hops(s[0]))
    ]
    scale = 1.0 / total

    def load(k):
        columns = pl.ds(pl.multiple_of(k * width, width), width)
        return pltpu.make_async_copy(jac_hbm.at[:, columns], jac.at[:, columns], load_sem.at[k])

    for k in range(CHUNKS):
        load(k).start()

    barrier = pltpu.get_barrier_semaphore()
    others = [
        device((x + a) % 4, (y + b) % 4, z, 1 - c) for a in range(4) for b in range(4) if a or b
    ]
    greeted = plane_peers + others + [peer for _, peer in column_peers]
    for peer in greeted:
        pl.semaphore_signal(barrier, inc=1, device_id=peer, device_id_type=MESH)
    pl.semaphore_wait(barrier, len(greeted))

    def copy_to(peer, source, target, send, recv):
        return pltpu.make_async_remote_copy(
            source, target, send, recv, device_id=peer, device_id_type=MESH
        )

    def column_copy(p, k, core, peer):
        return copy_to(
            peer, column_out.at[p, k, core], column.at[p, k, own], column_send.at[p, k], column_recv.at[p, k]
        )

    def column_all(p, k):
        some = column.at[p, k, pl.ds(0, 7)]
        return copy_to(sibling, some, some, column_send.at[p, k], column_recv.at[p, k])

    def plane_copy(p, k, slot, peer):
        piece = plane.at[p, k, slot]
        return copy_to(peer, piece, piece, plane_send.at[p, k], plane_recv.at[p, k])

    def plane_all(p, k):
        return plane_copy(p, k, pl.ds(0, 15), sibling)

    def core_copy(p, k):
        piece = image.at[p, pl.ds(k * tall + c * half, half)]
        return copy_to(sibling, piece, piece, core_send.at[p, k], core_recv.at[p, k])

    def each(step):
        lax.fori_loop(0, CHUNKS, lambda k, _: (step(k), 0)[1], 0)

    def multiply(k, vector):
        base = pl.multiple_of(k * width, width)
        split = tall - VECTOR_TILES
        product = jnp.dot(vector, jac[:, pl.ds(base, split * LANES)], preferred_element_type=f32)
        for i in range(split):
            part[i : i + 1] = product[:1, i * LANES : (i + 1) * LANES]
        sums = [jnp.zeros((8, LANES), f32) for _ in range(VECTOR_TILES)]
        for r in range(0, rows, 8):
            factor = spread[r : r + 8]
            for w in range(VECTOR_TILES):
                columns = pl.ds(base + (split + w) * LANES, LANES)
                sums[w] += jac[r : r + 8, columns].astype(f32) * factor
        for w in range(VECTOR_TILES):
            part[split + w : split + w + 1] = jnp.sum(sums[w], axis=0, keepdims=True)

    def transpose(first, count):
        piece = 512

        def one(i, _):
            columns = pl.ds(pl.multiple_of(i * piece, piece), piece)
            jac_t[columns, :] = jac[:, columns].T
            return 0

        lax.fori_loop(first // piece, (first + count) // piece, one, 0)

    def send_columns(p, row, first):
        vector = jnp.broadcast_to(row, (8, rows)).astype(bf16)
        whole = vector[:1].astype(f32)
        for i in range(rows // LANES):
            tile = jnp.broadcast_to(whole[:, i * LANES : (i + 1) * LANES], (LANES, LANES))
            spread[i * LANES : (i + 1) * LANES] = tile.T

        def chunk(k):
            if first:
                load(k).wait()
            multiply(k, vector)
            column_out[p, k, 0] = part[:half].astype(bf16)
            column_out[p, k, 1] = part[half:].astype(bf16)
            column[p, k, own] = column_out[p, k, c]
            for core, peer in column_peers:
                column_copy(p, k, core, peer).start()

        each(chunk)

    def column_sum(p, k):
        column_all(p, k).wait_recv()
        return jnp.sum(column[p, k].astype(f32), axis=0).astype(bf16)

    def send_plane(p, k):
        plane[p, k, me] = column_sum(p, k)
        for peer in plane_peers:
            plane_copy(p, k, me, peer).start()

    def forward(p, k, h):
        value = image[p, pl.ds(k * tall + h * half, half)]
        high = value.astype(bf16).astype(f32)
        wide[0] = high
        wide[1] = value - high
        for i in range(half):
            columns = slice(i * LANES, (i + 1) * LANES)
            narrow[0:1, columns] = wide[0, i : i + 1]
            narrow[1:2, columns] = wide[1, i : i + 1]
        depth = width // 2
        base = pl.multiple_of(k * width + h * depth, depth)
        out = jnp.dot(narrow[...].astype(bf16), jac_t[pl.ds(base, depth), :], preferred_element_type=f32)
        return out[0:1] + out[1:2]

    def gather(p):
        def mine(k, inner):
            plane_all(p, k).wait_recv()
            value = jnp.sum(plane[p, k].astype(f32), axis=0)
            image[p, pl.ds(k * tall + c * half, half)] = value * scale
            core_copy(p, k).start()
            return inner + forward(p, k, c)

        def theirs(k, inner):
            core_copy(p, k).wait_recv()
            return inner + forward(p, k, 1 - c)

        inner = lax.fori_loop(0, CHUNKS, mine, jnp.zeros((1, rows), f32))
        return lax.fori_loop(0, CHUNKS, theirs, inner)

    def drain(p):
        def chunk(k):
            column_all(p, k).wait_send()
            plane_all(p, k).wait_send()
            core_copy(p, k).wait_send()

        each(chunk)

    def dot(a, b):
        return jnp.sum(a * b, keepdims=True)

    narrow[...] = jnp.zeros(narrow.shape, f32)
    start = lax.axis_index("par") * (rows // LANES)
    deviation = jnp.concatenate(
        [energy[pl.ds(start + i, 1), :] for i in range(rows // LANES)], axis=1
    )
    send_columns(0, deviation, True)
    transpose(0, params // 2)
    each(functools.partial(send_plane, 0))
    transpose(params // 2, params // 2)
    inner = gather(0)
    drain(0)
    force = image[0]
    residual[...] = force
    direction[...] = force
    update[...] = jnp.zeros(force.shape, f32)
    norm = dot(force, force)

    def step(it, carry):
        norm, left, along = carry
        p = (it + 1) % 2
        send_columns(p, along, False)
        each(functools.partial(send_plane, p))
        inner = gather(p) + DAMPING * along
        drain(p)
        applied = image[p] + DAMPING * direction[...]
        alpha = norm / dot(direction[...], applied)
        update[...] = update[...] + alpha * direction[...]
        residual[...] = residual[...] - alpha * applied
        new = dot(residual[...], residual[...])
        beta = new / norm
        direction[...] = residual[...] + beta * direction[...]
        left = left - alpha * inner
        return new, left, left + beta * along

    norm, left, along = lax.fori_loop(0, ITERS - 1, step, (norm, inner, inner))

    p = ITERS % 2

    def scalar_copy(buffer, slot, stage, peer):
        piece = buffer.at[slot]
        return copy_to(peer, piece, piece, scalar_send.at[stage], scalar_recv.at[stage])

    squares = dot(along.astype(bf16).astype(f32), along)
    scalar_column[own] = jnp.broadcast_to(squares, (1, LANES))
    for _, peer in column_peers:
        scalar_copy(scalar_column, own, 0, peer).start()
    send_columns(p, along, False)
    scalar_copy(scalar_column, pl.ds(0, 7), 0, sibling).wait()
    scalar_plane[me] = jnp.sum(scalar_column[...], axis=0)
    for peer in plane_peers:
        scalar_copy(scalar_plane, me, 1, peer).start()

    def last_copy(source, slot, peer):
        return copy_to(peer, source, last.at[slot], last_send, last_recv)

    for k in range(CHUNKS):
        last_out[k] = column_sum(p, k)
        to_y = 2 * (k % 2) + c
        for to_x in (k // 2, k // 2 + 2):
            last_copy(last_out.at[k], me, device(to_x, to_y, z, 1 - c)).start()
            local = jnp.logical_and(x == to_x, y == to_y)

            @pl.when(jnp.logical_not(local))
            def _():
                last_copy(last_out.at[k], me, device(to_x, to_y, z, c)).start()

            @pl.when(local)
            def _():
                last[me] = last_out[k]

    scalar_copy(scalar_plane, pl.ds(0, 15), 1, sibling).wait()
    squares = jnp.sum(scalar_plane[...], axis=0)[:, :1] * scale
    alpha = norm / (squares + DAMPING * dot(direction[...], direction[...]))

    def last_all(count):
        return last_copy(last.at[pl.ds(0, count)], pl.ds(0, count), sibling)

    inside = y % 2 == c

    @pl.when(inside)
    def _():
        last_all(15).wait_recv()

    @pl.when(jnp.logical_not(inside))
    def _():
        last_all(16).wait_recv()

    value = jnp.sum(last[...].astype(f32), axis=0) * scale
    mine = pl.ds(lax.axis_index("par") * half, half)
    outs[0] = update[mine] + alpha * direction[mine]
    outs[1] = residual[mine] - alpha * (value + DAMPING * direction[mine])

    each(lambda k: column_all(p, k).wait_send())

    @pl.when(inside)
    def _():
        last_all(15).wait_send()

    @pl.when(jnp.logical_not(inside))
    def _():
        last_all(16).wait_send()


def body(jacobian, energy):
    rows, params = jacobian.shape
    total = rows * lax.axis_size("samp") * lax.axis_size("par")
    tall = params // CHUNKS // LANES
    whole = (params // LANES, LANES)
    piece = (tall // 2, LANES)
    vmem = pl.BlockSpec(memory_space=pltpu.VMEM)
    dma = pltpu.SemaphoreType.DMA
    outs = pl.pallas_call(
        functools.partial(kernel, total),
        out_shape=pltpu.VMEM((2, *piece), f32),
        in_specs=[vmem, pl.BlockSpec(memory_space=pl.ANY)],
        out_specs=vmem,
        scratch_shapes=[
            pltpu.VMEM((rows, params), bf16),
            pltpu.VMEM((params, rows), bf16),
            pltpu.VMEM((tall, LANES), f32),
            pltpu.VMEM((rows, LANES), f32),
            pltpu.VMEM((2, CHUNKS, 2, *piece), bf16),
            pltpu.VMEM((2, CHUNKS, 8, *piece), bf16),
            pltpu.VMEM((2, CHUNKS, 16, *piece), bf16),
            pltpu.VMEM((CHUNKS, *piece), bf16),
            pltpu.VMEM((16, *piece), bf16),
            pltpu.VMEM((8, 1, LANES), f32),
            pltpu.VMEM((16, 1, LANES), f32),
            pltpu.VMEM(whole, f32),
            pltpu.VMEM(whole, f32),
            pltpu.VMEM(whole, f32),
            pltpu.VMEM((2, *whole), f32),
            pltpu.VMEM((2, *piece), f32),
            pltpu.VMEM((8, params // CHUNKS // 2), f32),
            dma((CHUNKS,)),
        ]
        + [dma((2, CHUNKS))] * 6
        + [dma, dma, dma((2,)), dma((2,))],
        compiler_params=pltpu.CompilerParams(
            collective_id=0, has_side_effects=True, vmem_limit_bytes=56 * 2**20
        ),
    )(energy.reshape(-1, LANES), jacobian)
    return outs[0].reshape(-1), outs[1].reshape(-1)


def solution(mesh):
    return jax.shard_map(
        body,
        mesh=mesh,
        in_specs=(P(("samp", "par"), None), P("samp")),
        out_specs=(P("par"), P("par")),
        check_vma=False,
    )
```

```python
import functools

import jax
import jax.numpy as jnp
from jax import lax
from jax.experimental import pallas as pl
from jax.experimental.pallas import tpu as pltpu
from jax.sharding import PartitionSpec as P

ITERS = 3
DAMPING = 0.05
LANES = 128
CHUNKS = 4
MESH = pl.DeviceIdType.MESH
f32, bf16 = jnp.float32, jnp.bfloat16


def coordinates():
    samp, par = lax.axis_index("samp"), lax.axis_index("par")
    x = (samp // 8) * 2 + par // 4
    return x, par % 4, (samp // 2) % 4, samp % 2


def device(x, y, z, c):
    return ((x // 2) * 8 + z * 2 + c, (x % 2) * 4 + y)


def hops(*steps):
    return -sum(min(s, 4 - s) for s in steps)


def kernel(
    total,
    energy, jac_hbm, outs,
    jac, jac_t, part, column_out, column, plane, last_out, last, scalar_column, scalar_plane,
    update, residual, direction, image, wide, narrow,
    load_sem, column_send, column_recv, plane_send, plane_recv, core_send, core_recv,
    last_send, last_recv, scalar_send, scalar_recv,
):
    rows, params = jac.shape
    width = params // CHUNKS
    tall = width // LANES
    half = tall // 2
    x, y, z, c = coordinates()
    me = x * 4 + y
    own = c * 4 + z
    sibling = device(x, y, z, 1 - c)
    plane_peers = [
        device((x + a) % 4, (y + b) % 4, z, c)
        for a, b in sorted(((a, b) for a in range(4) for b in range(4) if a or b), key=lambda s: hops(*s))
    ]
    column_peers = [
        ((c + e) % 2, device(x, y, (z + d) % 4, (c + e) % 2))
        for d, e in sorted(((d, e) for d in range(4) for e in range(2) if d or e), key=lambda s: hops(s[0]))
    ]
    scale = 1.0 / total

    def load(k):
        columns = pl.ds(pl.multiple_of(k * width, width), width)
        return pltpu.make_async_copy(jac_hbm.at[:, columns], jac.at[:, columns], load_sem.at[k])

    for k in range(CHUNKS):
        load(k).start()

    barrier = pltpu.get_barrier_semaphore()
    others = [
        device((x + a) % 4, (y + b) % 4, z, 1 - c) for a in range(4) for b in range(4) if a or b
    ]
    greeted = plane_peers + others + [peer for _, peer in column_peers]
    for peer in greeted:
        pl.semaphore_signal(barrier, inc=1, device_id=peer, device_id_type=MESH)
    pl.semaphore_wait(barrier, len(greeted))

    def copy_to(peer, source, target, send, recv):
        return pltpu.make_async_remote_copy(
            source, target, send, recv, device_id=peer, device_id_type=MESH
        )

    def column_copy(p, k, core, peer):
        return copy_to(
            peer, column_out.at[p, k, core], column.at[p, k, own], column_send.at[p, k], column_recv.at[p, k]
        )

    def column_all(p, k):
        some = column.at[p, k, pl.ds(0, 7)]
        return copy_to(sibling, some, some, column_send.at[p, k], column_recv.at[p, k])

    def plane_copy(p, k, slot, peer):
        piece = plane.at[p, k, slot]
        return copy_to(peer, piece, piece, plane_send.at[p, k], plane_recv.at[p, k])

    def plane_all(p, k):
        return plane_copy(p, k, pl.ds(0, 15), sibling)

    def core_copy(p, k):
        piece = image.at[p, pl.ds(k * tall + c * half, half)]
        return copy_to(sibling, piece, piece, core_send.at[p, k], core_recv.at[p, k])

    def each(step):
        lax.fori_loop(0, CHUNKS, lambda k, _: (step(k), 0)[1], 0)

    def multiply(k, vector):
        columns = pl.ds(k * width, width)
        product = jnp.dot(vector, jac[:, columns], preferred_element_type=f32)
        for i in range(tall):
            part[i : i + 1] = product[:1, i * LANES : (i + 1) * LANES]

    def transpose(first, count):
        piece = 512

        def one(i, _):
            columns = pl.ds(pl.multiple_of(first + i * piece, piece), piece)
            jac_t[columns, :] = jac[:, columns].T
            return 0

        lax.fori_loop(0, count // piece, one, 0)

    def send_columns(p, row, first):
        vector = jnp.broadcast_to(row, (8, rows)).astype(bf16)

        def chunk(k):
            if first:
                load(k).wait()
            multiply(k, vector)
            column_out[p, k, 0] = part[:half].astype(bf16)
            column_out[p, k, 1] = part[half:].astype(bf16)
            column[p, k, own] = column_out[p, k, c]
            for core, peer in column_peers:
                column_copy(p, k, core, peer).start()

        for k in range(CHUNKS):
            chunk(k)

    def column_sum(p, k):
        column_all(p, k).wait_recv()
        return jnp.sum(column[p, k].astype(f32), axis=0).astype(bf16)

    def send_plane(p, k):
        plane[p, k, me] = column_sum(p, k)
        for peer in plane_peers:
            plane_copy(p, k, me, peer).start()

    def forward(p, k, h):
        value = image[p, pl.ds(k * tall + h * half, half)]
        high = value.astype(bf16).astype(f32)
        wide[0] = high
        wide[1] = value - high
        for i in range(half):
            columns = slice(i * LANES, (i + 1) * LANES)
            narrow[0:1, columns] = wide[0, i : i + 1]
            narrow[1:2, columns] = wide[1, i : i + 1]
        depth = width // 2
        base = pl.multiple_of(k * width + h * depth, depth)
        out = jnp.dot(narrow[...].astype(bf16), jac_t[pl.ds(base, depth), :], preferred_element_type=f32)
        return out[0:1] + out[1:2]

    def gather(p):
        lag = 2

        def mine(k, inner):
            plane_all(p, k).wait_recv()
            value = jnp.sum(plane[p, k].astype(f32), axis=0)
            image[p, pl.ds(k * tall + c * half, half)] = value * scale
            core_copy(p, k).start()
            return inner + forward(p, k, c)

        def theirs(k, inner):
            core_copy(p, k).wait_recv()
            return inner + forward(p, k, 1 - c)

        inner = lax.fori_loop(0, lag, mine, jnp.zeros((1, rows), f32))
        inner = lax.fori_loop(lag, CHUNKS, lambda k, sum: theirs(k - lag, mine(k, sum)), inner)
        return lax.fori_loop(CHUNKS - lag, CHUNKS, theirs, inner)

    def drain(p):
        def chunk(k):
            column_all(p, k).wait_send()
            plane_all(p, k).wait_send()
            core_copy(p, k).wait_send()

        each(chunk)

    def dot(a, b):
        return jnp.sum(a * b, keepdims=True)

    narrow[...] = jnp.zeros(narrow.shape, f32)
    start = lax.axis_index("par") * (rows // LANES)
    deviation = jnp.concatenate(
        [energy[pl.ds(start + i, 1), :] for i in range(rows // LANES)], axis=1
    )
    update[...] = jnp.zeros(update.shape, f32)
    direction[...] = jnp.zeros(direction.shape, f32)
    send_columns(0, deviation, True)

    def first_plane(k):
        send_plane(0, k)
        transpose(k * width, width)

    each(first_plane)
    inner = gather(0)
    force = image[0]
    residual[...] = force
    norm = dot(force, force)

    def settle(p, alpha, beta):
        update[...] = update[...] + alpha * direction[...]
        direction[...] = residual[...] + beta * direction[...]
        drain(p)

    def step(it, carry):
        norm, alpha, beta, left, along = carry
        p = (it + 1) % 2
        send_columns(p, along, False)
        settle(1 - p, alpha, beta)
        each(functools.partial(send_plane, p))
        inner = gather(p) + DAMPING * along
        applied = image[p] + DAMPING * direction[...]
        alpha = norm / dot(direction[...], applied)
        rest = residual[...] - alpha * applied
        residual[...] = rest
        new = dot(rest, rest)
        beta = new / norm
        left = left - alpha * inner
        return new, alpha, beta, left, left + beta * along

    zero = jnp.zeros((1, 1), f32)
    norm, alpha, beta, left, along = lax.fori_loop(0, ITERS - 1, step, (norm, zero, zero, inner, inner))

    p = ITERS % 2

    def scalar_copy(buffer, slot, stage, peer):
        piece = buffer.at[slot]
        return copy_to(peer, piece, piece, scalar_send.at[stage], scalar_recv.at[stage])

    squares = dot(along.astype(bf16).astype(f32), along)
    scalar_column[own] = jnp.broadcast_to(squares, (1, LANES))
    for _, peer in column_peers:
        scalar_copy(scalar_column, own, 0, peer).start()
    send_columns(p, along, False)
    settle(1 - p, alpha, beta)
    scalar_copy(scalar_column, pl.ds(0, 7), 0, sibling).wait()
    scalar_plane[me] = jnp.sum(scalar_column[...], axis=0)
    for peer in plane_peers:
        scalar_copy(scalar_plane, me, 1, peer).start()

    def last_copy(source, slot, peer):
        return copy_to(peer, source, last.at[slot], last_send, last_recv)

    for k in range(CHUNKS):
        last_out[k] = column_sum(p, k)
        to_y = 2 * (k % 2) + c
        for to_x in (k // 2, k // 2 + 2):
            last_copy(last_out.at[k], me, device(to_x, to_y, z, 1 - c)).start()
            local = jnp.logical_and(x == to_x, y == to_y)

            @pl.when(jnp.logical_not(local))
            def _():
                last_copy(last_out.at[k], me, device(to_x, to_y, z, c)).start()

            @pl.when(local)
            def _():
                last[me] = last_out[k]

    scalar_copy(scalar_plane, pl.ds(0, 15), 1, sibling).wait()
    squares = jnp.sum(scalar_plane[...], axis=0)[:, :1] * scale
    alpha = norm / (squares + DAMPING * dot(direction[...], direction[...]))

    def last_all(count):
        return last_copy(last.at[pl.ds(0, count)], pl.ds(0, count), sibling)

    inside = y % 2 == c

    @pl.when(inside)
    def _():
        last_all(15).wait_recv()

    @pl.when(jnp.logical_not(inside))
    def _():
        last_all(16).wait_recv()

    value = jnp.sum(last[...].astype(f32), axis=0) * scale
    mine = pl.ds(lax.axis_index("par") * half, half)
    outs[0] = update[mine] + alpha * direction[mine]
    outs[1] = residual[mine] - alpha * (value + DAMPING * direction[mine])

    each(lambda k: column_all(p, k).wait_send())

    @pl.when(inside)
    def _():
        last_all(15).wait_send()

    @pl.when(jnp.logical_not(inside))
    def _():
        last_all(16).wait_send()


def body(jacobian, energy):
    rows, params = jacobian.shape
    total = rows * lax.axis_size("samp") * lax.axis_size("par")
    tall = params // CHUNKS // LANES
    whole = (params // LANES, LANES)
    piece = (tall // 2, LANES)
    vmem = pl.BlockSpec(memory_space=pltpu.VMEM)
    dma = pltpu.SemaphoreType.DMA
    outs = pl.pallas_call(
        functools.partial(kernel, total),
        out_shape=pltpu.VMEM((2, *piece), f32),
        in_specs=[vmem, pl.BlockSpec(memory_space=pl.ANY)],
        out_specs=vmem,
        scratch_shapes=[
            pltpu.VMEM((rows, params), bf16),
            pltpu.VMEM((params, rows), bf16),
            pltpu.VMEM((tall, LANES), f32),
            pltpu.VMEM((2, CHUNKS, 2, *piece), bf16),
            pltpu.VMEM((2, CHUNKS, 8, *piece), bf16),
            pltpu.VMEM((2, CHUNKS, 16, *piece), bf16),
            pltpu.VMEM((CHUNKS, *piece), bf16),
            pltpu.VMEM((16, *piece), bf16),
            pltpu.VMEM((8, 1, LANES), f32),
            pltpu.VMEM((16, 1, LANES), f32),
            pltpu.VMEM(whole, f32),
            pltpu.VMEM(whole, f32),
            pltpu.VMEM(whole, f32),
            pltpu.VMEM((2, *whole), f32),
            pltpu.VMEM((2, *piece), f32),
            pltpu.VMEM((8, params // CHUNKS // 2), f32),
            dma((CHUNKS,)),
        ]
        + [dma((2, CHUNKS))] * 6
        + [dma, dma, dma((2,)), dma((2,))],
        compiler_params=pltpu.CompilerParams(
            collective_id=0, has_side_effects=True, vmem_limit_bytes=56 * 2**20
        ),
    )(energy.reshape(-1, LANES), jacobian)
    return outs[0].reshape(-1), outs[1].reshape(-1)


def solution(mesh):
    return jax.shard_map(
        body,
        mesh=mesh,
        in_specs=(P(("samp", "par"), None), P("samp")),
        out_specs=(P("par"), P("par")),
        check_vma=False,
    )
```

```python
import functools

import jax
import jax.numpy as jnp
from jax import lax
from jax.experimental import pallas as pl
from jax.experimental.pallas import tpu as pltpu
from jax.sharding import PartitionSpec as P

ITERS = 3
DAMPING = 0.05
LANES = 128
CHUNKS = 4
MESH = pl.DeviceIdType.MESH
f32, bf16 = jnp.float32, jnp.bfloat16


def coordinates():
    samp, par = lax.axis_index("samp"), lax.axis_index("par")
    x = (samp // 8) * 2 + par // 4
    return x, par % 4, (samp // 2) % 4, samp % 2


def device(x, y, z, c):
    return ((x // 2) * 8 + z * 2 + c, (x % 2) * 4 + y)


def hops(*steps):
    return -sum(min(s, 4 - s) for s in steps)


def kernel(
    total,
    energy_hbm, jac_hbm, outs,
    energy, jac, jac_t, part, column_out, column, plane, cross, last_out, last, scalar_column, scalar_plane,
    update, residual, direction, image, wide, narrow,
    energy_sem, load_sem, column_send, column_recv, plane_send, plane_recv, core_send, core_recv,
    cross_send, cross_recv, last_send, last_recv, scalar_send, scalar_recv,
):
    rows, params = jac.shape
    width = params // CHUNKS
    tall = width // LANES
    half = tall // 2
    x, y, z, c = coordinates()
    me = x * 4 + y
    own = c * 4 + z
    sibling = device(x, y, z, 1 - c)
    plane_peers = [
        device((x + a) % 4, (y + b) % 4, z, c)
        for a, b in sorted(((a, b) for a in range(4) for b in range(4) if a or b), key=lambda s: hops(*s))
    ]
    column_peers = [
        ((c + e) % 2, device(x, y, (z + d) % 4, (c + e) % 2))
        for d, e in sorted(((d, e) for d in range(4) for e in range(2) if d or e), key=lambda s: hops(s[0]))
    ]
    scale = 1.0 / total

    def load(i):
        columns = pl.ds(i * width, width)
        return pltpu.make_async_copy(jac_hbm.at[:, columns], jac.at[:, columns], load_sem.at[i])

    load_energy = pltpu.make_async_copy(energy_hbm, energy, energy_sem)
    load_energy.start()
    for i in range(CHUNKS):
        load(i).start()

    barrier = pltpu.get_barrier_semaphore()
    others = [
        device((x + a) % 4, (y + b) % 4, z, 1 - c)
        for a, b in sorted(((a, b) for a in range(4) for b in range(4) if a or b), key=lambda s: hops(*s))
    ]
    greeted = plane_peers + others + [peer for _, peer in column_peers]
    for peer in greeted:
        pl.semaphore_signal(barrier, inc=1, device_id=peer, device_id_type=MESH)
    pl.semaphore_wait(barrier, len(greeted))

    def copy_to(peer, source, target, send, recv):
        return pltpu.make_async_remote_copy(
            source, target, send, recv, device_id=peer, device_id_type=MESH
        )

    def column_copy(p, k, core, peer):
        return copy_to(
            peer, column_out.at[p, k, core], column.at[p, k, own], column_send.at[p, k], column_recv.at[p, k]
        )

    def column_all(p, k):
        some = column.at[p, k, pl.ds(0, 7)]
        return copy_to(sibling, some, some, column_send.at[p, k], column_recv.at[p, k])

    def plane_copy(p, k, slot, peer):
        piece = plane.at[p, k, slot]
        return copy_to(peer, piece, piece, plane_send.at[p, k], plane_recv.at[p, k])

    def plane_all(p, k):
        return plane_copy(p, k, pl.ds(0, 15), sibling)

    def core_copy(p, k):
        piece = image.at[p, pl.ds(k * tall + c * half, half)]
        return copy_to(sibling, piece, piece, core_send.at[p, k], core_recv.at[p, k])

    def cross_copy(slot, source, peer):
        return copy_to(peer, source, cross.at[slot], cross_send, cross_recv)

    def each(step):
        lax.fori_loop(0, CHUNKS, lambda k, _: (step(k), 0)[1], 0)

    def multiply(k, h, count, vector):
        columns = pl.ds(k * width + h * width // 2, count * width // 2)
        product = jnp.dot(vector, jac[:, columns], preferred_element_type=f32)
        for i in range(count * half):
            part[h * half + i : h * half + i + 1] = product[:1, i * LANES : (i + 1) * LANES]

    def transpose(first, count):
        piece = 512

        def one(i, _):
            columns = pl.ds(pl.multiple_of(first + i * piece, piece), piece)
            jac_t[columns, :] = jac[:, columns].T
            return 0

        lax.fori_loop(0, count // piece, one, 0)

    def send_columns(p, row, first, between=None):
        vector = jnp.broadcast_to(row, (8, rows)).astype(bf16)
        for k in range(CHUNKS):
            if first:
                load(k).wait()
            multiply(k, 0, 2, vector)
            column_out[p, k, 0] = part[:half].astype(bf16)
            column_out[p, k, 1] = part[half:].astype(bf16)
            column[p, k, own] = column_out[p, k, c]
            for core, peer in column_peers:
                column_copy(p, k, core, peer).start()
            if first and k < CHUNKS - 1:
                transpose(3 * k * params // 32, 3 * params // 32)
            if between is not None and k == 0:
                between()

    def column_sum(p, k):
        column_all(p, k).wait_recv()
        return jnp.sum(column[p, k].astype(f32), axis=0).astype(bf16)

    def send_plane(p, k):
        plane[p, k, me] = column_sum(p, k)
        for peer in plane_peers:
            plane_copy(p, k, me, peer).start()

    def forward(p, k, h):
        value = image[p, pl.ds(k * tall + h * half, half)]
        high = value.astype(bf16).astype(f32)
        wide[0] = high
        wide[1] = value - high
        for i in range(half):
            columns = slice(i * LANES, (i + 1) * LANES)
            narrow[0:1, columns] = wide[0, i : i + 1]
            narrow[1:2, columns] = wide[1, i : i + 1]
        depth = width // 2
        base = pl.multiple_of(k * width + h * depth, depth)
        out = jnp.dot(narrow[...].astype(bf16), jac_t[pl.ds(base, depth), :], preferred_element_type=f32)
        return out[0:1] + out[1:2]

    def mine(p, k, inner, exchange=True):
        plane_all(p, k).wait_recv()
        value = jnp.sum(plane[p, k].astype(f32), axis=0)
        image[p, pl.ds(k * tall + c * half, half)] = value * scale
        if exchange:
            core_copy(p, k).start()
        return inner + forward(p, k, c)

    def theirs(p, k, inner):
        core_copy(p, k).wait_recv()
        return inner + forward(p, k, 1 - c)

    def gather(p):
        lag = 2
        inner = lax.fori_loop(0, lag, functools.partial(mine, p), jnp.zeros((1, rows), f32))
        inner = lax.fori_loop(
            lag, CHUNKS, lambda k, sum: theirs(p, k - lag, mine(p, k, sum)), inner
        )
        return lax.fori_loop(CHUNKS - lag, CHUNKS, functools.partial(theirs, p), inner)

    def gather_first(p):
        k = CHUNKS - 1
        inner = mine(p, 0, jnp.zeros((1, rows), f32))
        inner = lax.fori_loop(1, k, lambda k, sum: theirs(p, k - 1, mine(p, k, sum)), inner)
        inner = mine(p, k, inner, False)
        inner = theirs(p, k - 1, inner)
        everything = pl.ds(0, 16)
        cross_copy(everything, cross.at[everything], sibling).wait()
        value = jnp.sum(cross[...].astype(f32), axis=0)
        image[p, pl.ds(k * tall + (1 - c) * half, half)] = value * scale
        return inner + forward(p, k, 1 - c)

    def drain(p, whole):
        def chunk(k):
            column_all(p, k).wait_send()
            plane_all(p, k).wait_send()

            @pl.when(jnp.logical_or(k < CHUNKS - 1, whole))
            def _():
                core_copy(p, k).wait_send()

        each(chunk)

    def dot(a, b):
        return jnp.sum(a * b, keepdims=True)

    narrow[...] = jnp.zeros(narrow.shape, f32)
    load_energy.wait()
    start = lax.axis_index("par") * (rows // LANES)
    deviation = jnp.concatenate(
        [energy[pl.ds(start + i, 1), :] for i in range(rows // LANES)], axis=1
    )
    update[...] = jnp.zeros(update.shape, f32)
    direction[...] = jnp.zeros(direction.shape, f32)
    send_columns(0, deviation, True)

    piece = params // 32
    send_plane(0, 0)
    transpose(9 * piece, 5 * piece)
    send_plane(0, 1)
    transpose(14 * piece, 5 * piece)
    send_plane(0, 2)
    transpose(19 * piece, 5 * piece)
    send_plane(0, 3)
    for peer in others + [sibling]:
        cross_copy(me, plane.at[0, 3, me], peer).start()
    transpose(24 * piece, 8 * piece)
    inner = gather_first(0)
    force = image[0]
    residual[...] = force
    norm = dot(force, force)

    def settle(p, alpha, beta, whole):
        update[...] = update[...] + alpha * direction[...]
        direction[...] = residual[...] + beta * direction[...]
        drain(p, whole)

    def step(it, carry):
        norm, alpha, beta, left, along = carry
        p = (it + 1) % 2
        send_columns(p, along, False)
        settle(1 - p, alpha, beta, it > 0)
        each(functools.partial(send_plane, p))
        inner = gather(p) + DAMPING * along
        applied = image[p] + DAMPING * direction[...]
        alpha = norm / dot(direction[...], applied)
        rest = residual[...] - alpha * applied
        residual[...] = rest
        new = dot(rest, rest)
        beta = new / norm
        left = left - alpha * inner
        return new, alpha, beta, left, left + beta * along

    zero = jnp.zeros((1, 1), f32)
    norm, alpha, beta, left, along = lax.fori_loop(0, ITERS - 1, step, (norm, zero, zero, inner, inner))

    p = ITERS % 2

    def scalar_copy(buffer, slot, stage, peer):
        piece = buffer.at[slot]
        return copy_to(peer, piece, piece, scalar_send.at[stage], scalar_recv.at[stage])

    def send_squares():
        squares = dot(along.astype(bf16).astype(f32), along)
        scalar_column[own] = jnp.broadcast_to(squares, (1, LANES))
        for _, peer in column_peers:
            scalar_copy(scalar_column, own, 0, peer).start()

    send_columns(p, along, False, send_squares)
    settle(1 - p, alpha, beta, True)
    scalar_copy(scalar_column, pl.ds(0, 7), 0, sibling).wait()
    scalar_plane[me] = jnp.sum(scalar_column[...], axis=0)
    for peer in plane_peers:
        scalar_copy(scalar_plane, me, 1, peer).start()

    def last_copy(source, slot, peer):
        return copy_to(peer, source, last.at[slot], last_send, last_recv)

    for k in range(CHUNKS):
        last_out[k] = column_sum(p, k)
        to_y = 2 * (k % 2) + c
        for to_x in (k // 2, k // 2 + 2):
            last_copy(last_out.at[k], me, device(to_x, to_y, z, 1 - c)).start()
            local = jnp.logical_and(x == to_x, y == to_y)

            @pl.when(jnp.logical_not(local))
            def _():
                last_copy(last_out.at[k], me, device(to_x, to_y, z, c)).start()

            @pl.when(local)
            def _():
                last[me] = last_out[k]

    scalar_copy(scalar_plane, pl.ds(0, 15), 1, sibling).wait()
    squares = jnp.sum(scalar_plane[...], axis=0)[:, :1] * scale
    alpha = norm / (squares + DAMPING * dot(direction[...], direction[...]))

    def last_all(count):
        return last_copy(last.at[pl.ds(0, count)], pl.ds(0, count), sibling)

    inside = y % 2 == c

    @pl.when(inside)
    def _():
        last_all(15).wait_recv()

    @pl.when(jnp.logical_not(inside))
    def _():
        last_all(16).wait_recv()

    value = jnp.sum(last[...].astype(f32), axis=0) * scale
    mine = pl.ds(lax.axis_index("par") * half, half)
    outs[0] = update[mine] + alpha * direction[mine]
    outs[1] = residual[mine] - alpha * (value + DAMPING * direction[mine])

    each(lambda k: column_all(p, k).wait_send())

    @pl.when(inside)
    def _():
        last_all(15).wait_send()

    @pl.when(jnp.logical_not(inside))
    def _():
        last_all(16).wait_send()


def body(jacobian, energy):
    rows, params = jacobian.shape
    total = rows * lax.axis_size("samp") * lax.axis_size("par")
    tall = params // CHUNKS // LANES
    whole = (params // LANES, LANES)
    piece = (tall // 2, LANES)
    vmem = pl.BlockSpec(memory_space=pltpu.VMEM)
    dma = pltpu.SemaphoreType.DMA
    outs = pl.pallas_call(
        functools.partial(kernel, total),
        out_shape=pltpu.VMEM((2, *piece), f32),
        in_specs=[pl.BlockSpec(memory_space=pltpu.HBM)] * 2,
        out_specs=vmem,
        scratch_shapes=[
            pltpu.VMEM((energy.shape[0] // LANES, LANES), f32),
            pltpu.VMEM((rows, params), bf16),
            pltpu.VMEM((params, rows), bf16),
            pltpu.VMEM((tall, LANES), f32),
            pltpu.VMEM((2, CHUNKS, 2, *piece), bf16),
            pltpu.VMEM((2, CHUNKS, 8, *piece), bf16),
            pltpu.VMEM((2, CHUNKS, 16, *piece), bf16),
            pltpu.VMEM((16, *piece), bf16),
            pltpu.VMEM((CHUNKS, *piece), bf16),
            pltpu.VMEM((16, *piece), bf16),
            pltpu.VMEM((8, 1, LANES), f32),
            pltpu.VMEM((16, 1, LANES), f32),
            pltpu.VMEM(whole, f32),
            pltpu.VMEM(whole, f32),
            pltpu.VMEM(whole, f32),
            pltpu.VMEM((2, *whole), f32),
            pltpu.VMEM((2, *piece), f32),
            pltpu.VMEM((8, params // CHUNKS // 2), f32),
            dma,
            dma((CHUNKS,)),
        ]
        + [dma((2, CHUNKS))] * 6
        + [dma, dma, dma, dma, dma((2,)), dma((2,))],
        compiler_params=pltpu.CompilerParams(
            collective_id=0, has_side_effects=True, vmem_limit_bytes=56 * 2**20
        ),
    )(energy.reshape(-1, LANES), jacobian)
    return outs[0].reshape(-1), outs[1].reshape(-1)


def solution(mesh):
    return jax.shard_map(
        body,
        mesh=mesh,
        in_specs=(P(("samp", "par"), None), P("samp")),
        out_specs=(P("par"), P("par")),
        check_vma=False,
    )
```

```python
import functools

import jax
import jax.numpy as jnp
from jax import lax
from jax.experimental import pallas as pl
from jax.experimental.pallas import tpu as pltpu
from jax.sharding import PartitionSpec as P

ITERS = 3
DAMPING = 0.05
LANES = 128
CHUNKS = 4
MESH = pl.DeviceIdType.MESH
f32, bf16 = jnp.float32, jnp.bfloat16


def coordinates():
    samp, par = lax.axis_index("samp"), lax.axis_index("par")
    x = (samp // 8) * 2 + par // 4
    return x, par % 4, (samp // 2) % 4, samp % 2


def device(x, y, z, c):
    return ((x // 2) * 8 + z * 2 + c, (x % 2) * 4 + y)


def hops(*steps):
    return -sum(min(s, 4 - s) for s in steps)


def kernel(
    total,
    energy_hbm, jac_hbm, outs,
    energy, jac, jac_t, part, column_out, column, plane, cross, last_out, last, scalar_column, scalar_plane,
    update, residual, direction, image, wide, narrow,
    energy_sem, load_sem, column_send, column_recv, plane_send, plane_recv, core_send, core_recv,
    cross_send, cross_recv, last_send, last_recv, scalar_send, scalar_recv,
):
    rows, params = jac.shape
    width = params // CHUNKS
    tall = width // LANES
    half = tall // 2
    x, y, z, c = coordinates()
    me = x * 4 + y
    own = c * 4 + z
    sibling = device(x, y, z, 1 - c)
    plane_peers = [
        device((x + a) % 4, (y + b) % 4, z, c)
        for a, b in sorted(((a, b) for a in range(4) for b in range(4) if a or b), key=lambda s: hops(*s))
    ]
    column_peers = [
        ((c + e) % 2, device(x, y, (z + d) % 4, (c + e) % 2))
        for d, e in sorted(((d, e) for d in range(4) for e in range(2) if d or e), key=lambda s: hops(s[0]))
    ]
    scale = 1.0 / total

    def load(i):
        columns = pl.ds(i * width, width)
        return pltpu.make_async_copy(jac_hbm.at[:, columns], jac.at[:, columns], load_sem.at[i])

    load_energy = pltpu.make_async_copy(energy_hbm, energy, energy_sem)
    load_energy.start()
    for i in range(2):
        load(i).start()

    barrier = pltpu.get_barrier_semaphore()
    others = [
        device((x + a) % 4, (y + b) % 4, z, 1 - c)
        for a, b in sorted(((a, b) for a in range(4) for b in range(4) if a or b), key=lambda s: hops(*s))
    ]
    greeted = plane_peers + others + [peer for _, peer in column_peers]
    for peer in greeted:
        pl.semaphore_signal(barrier, inc=1, device_id=peer, device_id_type=MESH)
    pl.semaphore_wait(barrier, len(greeted))

    def copy_to(peer, source, target, send, recv):
        return pltpu.make_async_remote_copy(
            source, target, send, recv, device_id=peer, device_id_type=MESH
        )

    def column_copy(p, k, core, peer):
        return copy_to(
            peer, column_out.at[p, k, core], column.at[p, k, own], column_send.at[p, k], column_recv.at[p, k]
        )

    def column_all(p, k):
        some = column.at[p, k, pl.ds(0, 7)]
        return copy_to(sibling, some, some, column_send.at[p, k], column_recv.at[p, k])

    def plane_copy(p, k, slot, peer):
        piece = plane.at[p, k, slot]
        return copy_to(peer, piece, piece, plane_send.at[p, k], plane_recv.at[p, k])

    def plane_all(p, k):
        return plane_copy(p, k, pl.ds(0, 15), sibling)

    def core_copy(p, k):
        piece = image.at[p, pl.ds(k * tall + c * half, half)]
        return copy_to(sibling, piece, piece, core_send.at[p, k], core_recv.at[p, k])

    def cross_copy(slot, source, peer):
        return copy_to(peer, source, cross.at[slot], cross_send, cross_recv)

    def each(step):
        lax.fori_loop(0, CHUNKS, lambda k, _: (step(k), 0)[1], 0)

    def multiply(k, h, count, vector):
        columns = pl.ds(k * width + h * width // 2, count * width // 2)
        product = jnp.dot(vector, jac[:, columns], preferred_element_type=f32)
        for i in range(count * half):
            part[h * half + i : h * half + i + 1] = product[:1, i * LANES : (i + 1) * LANES]

    def transpose(first, count):
        piece = 512

        def one(i, _):
            columns = pl.ds(pl.multiple_of(first + i * piece, piece), piece)
            jac_t[columns, :] = jac[:, columns].T
            return 0

        lax.fori_loop(0, count // piece, one, 0)

    def send_columns(p, row, first, between=None):
        vector = jnp.broadcast_to(row, (8, rows)).astype(bf16)
        for k in range(CHUNKS):
            if first:
                load(k).wait()
                if k + 2 < CHUNKS:
                    load(k + 2).start()
            multiply(k, 0, 2, vector)
            column_out[p, k, 0] = part[:half].astype(bf16)
            column_out[p, k, 1] = part[half:].astype(bf16)
            column[p, k, own] = column_out[p, k, c]
            for core, peer in column_peers:
                column_copy(p, k, core, peer).start()
            if between is not None and k == 0:
                between()

    def column_sum(p, k):
        column_all(p, k).wait_recv()
        return jnp.sum(column[p, k].astype(f32), axis=0).astype(bf16)

    def send_plane(p, k):
        plane[p, k, me] = column_sum(p, k)
        for peer in plane_peers:
            plane_copy(p, k, me, peer).start()

    def forward(p, k, h, transposed=True):
        value = image[p, pl.ds(k * tall + h * half, half)]
        high = value.astype(bf16).astype(f32)
        wide[0] = high
        wide[1] = value - high
        for i in range(half):
            columns = slice(i * LANES, (i + 1) * LANES)
            narrow[0:1, columns] = wide[0, i : i + 1]
            narrow[1:2, columns] = wide[1, i : i + 1]
        depth = width // 2
        base = pl.multiple_of(k * width + h * depth, depth)
        terms = narrow[...].astype(bf16)
        if transposed:
            out = jnp.dot(terms, jac_t[pl.ds(base, depth), :], preferred_element_type=f32)
        else:
            out = lax.dot_general(
                terms, jac[:, pl.ds(base, depth)], (((1,), (1,)), ((), ())), preferred_element_type=f32
            )
        return out[0:1] + out[1:2]

    def mine(p, k, inner, exchange=True, transposed=True):
        plane_all(p, k).wait_recv()
        value = jnp.sum(plane[p, k].astype(f32), axis=0)
        image[p, pl.ds(k * tall + c * half, half)] = value * scale
        if exchange:
            core_copy(p, k).start()
        return inner + forward(p, k, c, transposed)

    def theirs(p, k, inner, transposed=True):
        core_copy(p, k).wait_recv()
        return inner + forward(p, k, 1 - c, transposed)

    def gather(p):
        lag = 2
        inner = lax.fori_loop(0, lag, functools.partial(mine, p), jnp.zeros((1, rows), f32))
        inner = lax.fori_loop(
            lag, CHUNKS, lambda k, sum: theirs(p, k - lag, mine(p, k, sum)), inner
        )
        return lax.fori_loop(CHUNKS - lag, CHUNKS, functools.partial(theirs, p), inner)

    def gather_first(p):
        k = CHUNKS - 1
        inner = mine(p, 0, jnp.zeros((1, rows), f32), True, False)
        inner = mine(p, 1, inner, True, False)
        inner = theirs(p, 0, inner, False)
        inner = mine(p, 2, inner)
        inner = theirs(p, 1, inner, False)
        inner = mine(p, k, inner, False)
        inner = theirs(p, k - 1, inner)
        everything = pl.ds(0, 16)
        cross_copy(everything, cross.at[everything], sibling).wait()
        value = jnp.sum(cross[...].astype(f32), axis=0)
        image[p, pl.ds(k * tall + (1 - c) * half, half)] = value * scale
        return inner + forward(p, k, 1 - c)

    def drain(p, whole):
        def chunk(k):
            column_all(p, k).wait_send()
            plane_all(p, k).wait_send()

            @pl.when(jnp.logical_or(k < CHUNKS - 1, whole))
            def _():
                core_copy(p, k).wait_send()

        each(chunk)

    def dot(a, b):
        return jnp.sum(a * b, keepdims=True)

    narrow[...] = jnp.zeros(narrow.shape, f32)
    load_energy.wait()
    start = lax.axis_index("par") * (rows // LANES)
    deviation = jnp.concatenate(
        [energy[pl.ds(start + i, 1), :] for i in range(rows // LANES)], axis=1
    )
    update[...] = jnp.zeros(update.shape, f32)
    direction[...] = jnp.zeros(direction.shape, f32)
    send_columns(0, deviation, True)

    piece = width // 2
    send_plane(0, 0)
    transpose(2 * width + 0 * piece, piece)
    send_plane(0, 1)
    transpose(2 * width + 1 * piece, piece)
    send_plane(0, 2)
    transpose(2 * width + 2 * piece, piece)
    send_plane(0, 3)
    for peer in others + [sibling]:
        cross_copy(me, plane.at[0, 3, me], peer).start()
    transpose(2 * width + 3 * piece, piece)
    inner = gather_first(0)
    force = image[0]
    residual[...] = force
    norm = dot(force, force)

    def settle(p, alpha, beta, whole):
        update[...] = update[...] + alpha * direction[...]
        direction[...] = residual[...] + beta * direction[...]
        drain(p, whole)

    def step(it, carry):
        norm, alpha, beta, left, along = carry
        p = (it + 1) % 2
        send_columns(p, along, False)
        settle(1 - p, alpha, beta, it > 0)

        @pl.when(it == 0)
        def _():
            transpose(0, width)

        each(functools.partial(send_plane, p))

        @pl.when(it == 0)
        def _():
            transpose(width, width)

        inner = gather(p) + DAMPING * along
        applied = image[p] + DAMPING * direction[...]
        alpha = norm / dot(direction[...], applied)
        rest = residual[...] - alpha * applied
        residual[...] = rest
        new = dot(rest, rest)
        beta = new / norm
        left = left - alpha * inner
        return new, alpha, beta, left, left + beta * along

    zero = jnp.zeros((1, 1), f32)
    norm, alpha, beta, left, along = lax.fori_loop(0, ITERS - 1, step, (norm, zero, zero, inner, inner))

    p = ITERS % 2

    def scalar_copy(buffer, slot, stage, peer):
        piece = buffer.at[slot]
        return copy_to(peer, piece, piece, scalar_send.at[stage], scalar_recv.at[stage])

    def send_squares():
        squares = dot(along.astype(bf16).astype(f32), along)
        scalar_column[own] = jnp.broadcast_to(squares, (1, LANES))
        for _, peer in column_peers:
            scalar_copy(scalar_column, own, 0, peer).start()

    send_columns(p, along, False, send_squares)
    settle(1 - p, alpha, beta, True)
    scalar_copy(scalar_column, pl.ds(0, 7), 0, sibling).wait()
    scalar_plane[me] = jnp.sum(scalar_column[...], axis=0)
    for peer in plane_peers:
        scalar_copy(scalar_plane, me, 1, peer).start()

    def last_copy(source, slot, peer):
        return copy_to(peer, source, last.at[slot], last_send, last_recv)

    for k in range(CHUNKS):
        last_out[k] = column_sum(p, k)
        to_y = 2 * (k % 2) + c
        for to_x in (k // 2, k // 2 + 2):
            last_copy(last_out.at[k], me, device(to_x, to_y, z, 1 - c)).start()
            local = jnp.logical_and(x == to_x, y == to_y)

            @pl.when(jnp.logical_not(local))
            def _():
                last_copy(last_out.at[k], me, device(to_x, to_y, z, c)).start()

            @pl.when(local)
            def _():
                last[me] = last_out[k]

    scalar_copy(scalar_plane, pl.ds(0, 15), 1, sibling).wait()
    squares = jnp.sum(scalar_plane[...], axis=0)[:, :1] * scale
    alpha = norm / (squares + DAMPING * dot(direction[...], direction[...]))

    def last_all(count):
        return last_copy(last.at[pl.ds(0, count)], pl.ds(0, count), sibling)

    inside = y % 2 == c

    @pl.when(inside)
    def _():
        last_all(15).wait_recv()

    @pl.when(jnp.logical_not(inside))
    def _():
        last_all(16).wait_recv()

    value = jnp.sum(last[...].astype(f32), axis=0) * scale
    mine = pl.ds(lax.axis_index("par") * half, half)
    outs[0] = update[mine] + alpha * direction[mine]
    outs[1] = residual[mine] - alpha * (value + DAMPING * direction[mine])

    each(lambda k: column_all(p, k).wait_send())

    @pl.when(inside)
    def _():
        last_all(15).wait_send()

    @pl.when(jnp.logical_not(inside))
    def _():
        last_all(16).wait_send()


def body(jacobian, energy):
    rows, params = jacobian.shape
    total = rows * lax.axis_size("samp") * lax.axis_size("par")
    tall = params // CHUNKS // LANES
    whole = (params // LANES, LANES)
    piece = (tall // 2, LANES)
    vmem = pl.BlockSpec(memory_space=pltpu.VMEM)
    dma = pltpu.SemaphoreType.DMA
    outs = pl.pallas_call(
        functools.partial(kernel, total),
        out_shape=pltpu.VMEM((2, *piece), f32),
        in_specs=[pl.BlockSpec(memory_space=pltpu.HBM)] * 2,
        out_specs=vmem,
        scratch_shapes=[
            pltpu.VMEM((energy.shape[0] // LANES, LANES), f32),
            pltpu.VMEM((rows, params), bf16),
            pltpu.VMEM((params, rows), bf16),
            pltpu.VMEM((tall, LANES), f32),
            pltpu.VMEM((2, CHUNKS, 2, *piece), bf16),
            pltpu.VMEM((2, CHUNKS, 8, *piece), bf16),
            pltpu.VMEM((2, CHUNKS, 16, *piece), bf16),
            pltpu.VMEM((16, *piece), bf16),
            pltpu.VMEM((CHUNKS, *piece), bf16),
            pltpu.VMEM((16, *piece), bf16),
            pltpu.VMEM((8, 1, LANES), f32),
            pltpu.VMEM((16, 1, LANES), f32),
            pltpu.VMEM(whole, f32),
            pltpu.VMEM(whole, f32),
            pltpu.VMEM(whole, f32),
            pltpu.VMEM((2, *whole), f32),
            pltpu.VMEM((2, *piece), f32),
            pltpu.VMEM((8, params // CHUNKS // 2), f32),
            dma,
            dma((CHUNKS,)),
        ]
        + [dma((2, CHUNKS))] * 6
        + [dma, dma, dma, dma, dma((2,)), dma((2,))],
        compiler_params=pltpu.CompilerParams(
            collective_id=0, has_side_effects=True, vmem_limit_bytes=56 * 2**20
        ),
    )(energy.reshape(-1, LANES), jacobian)
    return outs[0].reshape(-1), outs[1].reshape(-1)


def solution(mesh):
    return jax.shard_map(
        body,
        mesh=mesh,
        in_specs=(P(("samp", "par"), None), P("samp")),
        out_specs=(P("par"), P("par")),
        check_vma=False,
    )
```

```python
import functools

import jax
import jax.numpy as jnp
from jax import lax
from jax.experimental import pallas as pl
from jax.experimental.pallas import tpu as pltpu
from jax.sharding import PartitionSpec as P

ITERS = 3
DAMPING = 0.05
LANES = 128
CHUNKS = 4
MESH = pl.DeviceIdType.MESH
f32, bf16 = jnp.float32, jnp.bfloat16


def coordinates():
    samp, par = lax.axis_index("samp"), lax.axis_index("par")
    x = (samp // 8) * 2 + par // 4
    return x, par % 4, (samp // 2) % 4, samp % 2


def device(x, y, z, c):
    return ((x // 2) * 8 + z * 2 + c, (x % 2) * 4 + y)


def hops(*steps):
    return -sum(min(s, 4 - s) for s in steps)


def kernel(
    total,
    energy_hbm, jac_hbm, outs,
    energy, jac, jac_t, part, column_out, column, plane, cross, last_out, last, scalar_column, scalar_plane,
    update, residual, direction, image, wide, narrow,
    energy_sem, load_sem, column_send, column_recv, plane_send, plane_recv, core_send, core_recv,
    cross_send, cross_recv, last_send, last_recv, scalar_send, scalar_recv,
):
    rows, params = jac.shape
    width = params // CHUNKS
    tall = width // LANES
    half = tall // 2
    x, y, z, c = coordinates()
    me = x * 4 + y
    own = c * 4 + z
    sibling = device(x, y, z, 1 - c)
    plane_peers = [
        device((x + a) % 4, (y + b) % 4, z, c)
        for a, b in sorted(((a, b) for a in range(4) for b in range(4) if a or b), key=lambda s: hops(*s))
    ]
    column_peers = [
        ((c + e) % 2, device(x, y, (z + d) % 4, (c + e) % 2))
        for d, e in sorted(((d, e) for d in range(4) for e in range(2) if d or e), key=lambda s: hops(s[0]))
    ]
    scale = 1.0 / total

    def load(i):
        columns = pl.ds(i * width, width)
        return pltpu.make_async_copy(jac_hbm.at[:, columns], jac.at[:, columns], load_sem.at[i])

    load_energy = pltpu.make_async_copy(energy_hbm, energy, energy_sem)
    load_energy.start()
    for i in range(2):
        load(i).start()

    barrier = pltpu.get_barrier_semaphore()
    others = [
        device((x + a) % 4, (y + b) % 4, z, 1 - c)
        for a, b in sorted(((a, b) for a in range(4) for b in range(4) if a or b), key=lambda s: hops(*s))
    ]
    greeted = plane_peers + others + [peer for _, peer in column_peers]
    for peer in greeted:
        pl.semaphore_signal(barrier, inc=1, device_id=peer, device_id_type=MESH)
    pl.semaphore_wait(barrier, len(greeted))

    def copy_to(peer, source, target, send, recv):
        return pltpu.make_async_remote_copy(
            source, target, send, recv, device_id=peer, device_id_type=MESH
        )

    def column_copy(p, k, core, peer):
        return copy_to(
            peer, column_out.at[p, k, core], column.at[p, k, own], column_send.at[p, k], column_recv.at[p, k]
        )

    def column_all(p, k):
        some = column.at[p, k, pl.ds(0, 7)]
        return copy_to(sibling, some, some, column_send.at[p, k], column_recv.at[p, k])

    def plane_copy(p, k, slot, peer):
        piece = plane.at[p, k, slot]
        return copy_to(peer, piece, piece, plane_send.at[p, k], plane_recv.at[p, k])

    def plane_all(p, k):
        return plane_copy(p, k, pl.ds(0, 15), sibling)

    def core_copy(p, k):
        piece = image.at[p, pl.ds(k * tall + c * half, half)]
        return copy_to(sibling, piece, piece, core_send.at[p, k], core_recv.at[p, k])

    def cross_copy(slot, source, peer):
        return copy_to(peer, source, cross.at[slot], cross_send, cross_recv)

    def each(step):
        lax.fori_loop(0, CHUNKS, lambda k, _: (step(k), 0)[1], 0)

    def multiply(k, h, count, vector):
        columns = pl.ds(k * width + h * width // 2, count * width // 2)
        product = jnp.dot(vector, jac[:, columns], preferred_element_type=f32)
        for i in range(count * half):
            part[h * half + i : h * half + i + 1] = product[:1, i * LANES : (i + 1) * LANES]

    def transpose(first, count):
        piece = 512

        def one(i, _):
            columns = pl.ds(pl.multiple_of(first + i * piece, piece), piece)
            jac_t[columns, :] = jac[:, columns].T
            return 0

        lax.fori_loop(0, count // piece, one, 0)

    def send_columns(p, row, first, between=None):
        vector = jnp.broadcast_to(row, (8, rows)).astype(bf16)
        for k in range(CHUNKS):
            if first:
                load(k).wait()
                if k + 2 < CHUNKS:
                    load(k + 2).start()
            multiply(k, 0, 2, vector)
            column_out[p, k, 0] = part[:half].astype(bf16)
            column_out[p, k, 1] = part[half:].astype(bf16)
            column[p, k, own] = column_out[p, k, c]
            for core, peer in column_peers:
                column_copy(p, k, core, peer).start()
            if between is not None and k == 0:
                between()

    def column_sum(p, k):
        column_all(p, k).wait_recv()
        return jnp.sum(column[p, k].astype(f32), axis=0).astype(bf16)

    def send_plane(p, k):
        plane[p, k, me] = column_sum(p, k)
        for peer in plane_peers:
            plane_copy(p, k, me, peer).start()

    def forward(p, k, h, transposed=True):
        value = image[p, pl.ds(k * tall + h * half, half)]
        high = value.astype(bf16).astype(f32)
        wide[0] = high
        wide[1] = value - high
        for i in range(half):
            columns = slice(i * LANES, (i + 1) * LANES)
            narrow[0:1, columns] = wide[0, i : i + 1]
            narrow[1:2, columns] = wide[1, i : i + 1]
        depth = width // 2
        base = pl.multiple_of(k * width + h * depth, depth)
        terms = narrow[...].astype(bf16)
        if transposed:
            out = jnp.dot(terms, jac_t[pl.ds(base, depth), :], preferred_element_type=f32)
        else:
            out = lax.dot_general(
                terms, jac[:, pl.ds(base, depth)], (((1,), (1,)), ((), ())), preferred_element_type=f32
            )
        return out[0:1] + out[1:2]

    def mine(p, k, inner, exchange=True, transposed=True):
        plane_all(p, k).wait_recv()
        value = jnp.sum(plane[p, k].astype(f32), axis=0)
        image[p, pl.ds(k * tall + c * half, half)] = value * scale
        if exchange:
            core_copy(p, k).start()
        return inner + forward(p, k, c, transposed)

    def theirs(p, k, inner, transposed=True):
        core_copy(p, k).wait_recv()
        return inner + forward(p, k, 1 - c, transposed)

    def gather(p):
        inner = jnp.zeros((1, rows), f32)
        lag = 1
        for k in range(CHUNKS + lag):
            if k < CHUNKS:
                inner = mine(p, k, inner)
            if k >= lag:
                inner = theirs(p, k - lag, inner)
        return inner

    def gather_first(p):
        k = CHUNKS - 1
        inner = mine(p, 0, jnp.zeros((1, rows), f32), True, False)
        inner = mine(p, 1, inner, True, False)
        inner = theirs(p, 0, inner, False)
        inner = mine(p, 2, inner)
        inner = theirs(p, 1, inner, False)
        inner = mine(p, k, inner, False)
        inner = theirs(p, k - 1, inner)
        everything = pl.ds(0, 16)
        cross_copy(everything, cross.at[everything], sibling).wait()
        value = jnp.sum(cross[...].astype(f32), axis=0)
        image[p, pl.ds(k * tall + (1 - c) * half, half)] = value * scale
        return inner + forward(p, k, 1 - c)

    def drain(p, whole):
        def chunk(k):
            column_all(p, k).wait_send()
            plane_all(p, k).wait_send()

            @pl.when(jnp.logical_or(k < CHUNKS - 1, whole))
            def _():
                core_copy(p, k).wait_send()

        each(chunk)

    def dot(a, b):
        return jnp.sum(a * b, keepdims=True)

    narrow[...] = jnp.zeros(narrow.shape, f32)
    load_energy.wait()
    start = lax.axis_index("par") * (rows // LANES)
    deviation = jnp.concatenate(
        [energy[pl.ds(start + i, 1), :] for i in range(rows // LANES)], axis=1
    )
    update[...] = jnp.zeros(update.shape, f32)
    direction[...] = jnp.zeros(direction.shape, f32)
    send_columns(0, deviation, True)

    piece = width // 2
    send_plane(0, 0)
    transpose(2 * width + 0 * piece, piece)
    send_plane(0, 1)
    transpose(2 * width + 1 * piece, piece)
    send_plane(0, 2)
    transpose(2 * width + 2 * piece, piece)
    send_plane(0, 3)
    for peer in others + [sibling]:
        cross_copy(me, plane.at[0, 3, me], peer).start()
    transpose(2 * width + 3 * piece, piece)
    inner = gather_first(0)
    force = image[0]
    residual[...] = force
    norm = dot(force, force)

    def settle(p, alpha, beta, whole):
        update[...] = update[...] + alpha * direction[...]
        direction[...] = residual[...] + beta * direction[...]
        drain(p, whole)

    def step(it, carry):
        norm, alpha, beta, left, along = carry
        p = (it + 1) % 2
        send_columns(p, along, False)
        settle(1 - p, alpha, beta, it > 0)

        @pl.when(it == 0)
        def _():
            transpose(0, width)

        for k in range(CHUNKS):
            send_plane(p, k)

        @pl.when(it == 0)
        def _():
            transpose(width, width)

        inner = gather(p) + DAMPING * along
        applied = image[p] + DAMPING * direction[...]
        alpha = norm / dot(direction[...], applied)
        rest = residual[...] - alpha * applied
        residual[...] = rest
        new = dot(rest, rest)
        beta = new / norm
        left = left - alpha * inner
        return new, alpha, beta, left, left + beta * along

    zero = jnp.zeros((1, 1), f32)
    norm, alpha, beta, left, along = lax.fori_loop(0, ITERS - 1, step, (norm, zero, zero, inner, inner))

    p = ITERS % 2

    def scalar_copy(buffer, slot, stage, peer):
        piece = buffer.at[slot]
        return copy_to(peer, piece, piece, scalar_send.at[stage], scalar_recv.at[stage])

    def send_squares():
        squares = dot(along.astype(bf16).astype(f32), along)
        scalar_column[own] = jnp.broadcast_to(squares, (1, LANES))
        for _, peer in column_peers:
            scalar_copy(scalar_column, own, 0, peer).start()

    send_columns(p, along, False, send_squares)
    settle(1 - p, alpha, beta, True)
    scalar_copy(scalar_column, pl.ds(0, 7), 0, sibling).wait()
    scalar_plane[me] = jnp.sum(scalar_column[...], axis=0)
    for peer in plane_peers:
        scalar_copy(scalar_plane, me, 1, peer).start()

    def last_copy(source, slot, peer):
        return copy_to(peer, source, last.at[slot], last_send, last_recv)

    for k in range(CHUNKS):
        last_out[k] = column_sum(p, k)
        to_y = 2 * (k % 2) + c
        for to_x in (k // 2, k // 2 + 2):
            last_copy(last_out.at[k], me, device(to_x, to_y, z, 1 - c)).start()
            local = jnp.logical_and(x == to_x, y == to_y)

            @pl.when(jnp.logical_not(local))
            def _():
                last_copy(last_out.at[k], me, device(to_x, to_y, z, c)).start()

            @pl.when(local)
            def _():
                last[me] = last_out[k]

    scalar_copy(scalar_plane, pl.ds(0, 15), 1, sibling).wait()
    squares = jnp.sum(scalar_plane[...], axis=0)[:, :1] * scale
    alpha = norm / (squares + DAMPING * dot(direction[...], direction[...]))

    def last_all(count):
        return last_copy(last.at[pl.ds(0, count)], pl.ds(0, count), sibling)

    inside = y % 2 == c

    @pl.when(inside)
    def _():
        last_all(15).wait_recv()

    @pl.when(jnp.logical_not(inside))
    def _():
        last_all(16).wait_recv()

    value = jnp.sum(last[...].astype(f32), axis=0) * scale
    mine = pl.ds(lax.axis_index("par") * half, half)
    outs[0] = update[mine] + alpha * direction[mine]
    outs[1] = residual[mine] - alpha * (value + DAMPING * direction[mine])

    each(lambda k: column_all(p, k).wait_send())

    @pl.when(inside)
    def _():
        last_all(15).wait_send()

    @pl.when(jnp.logical_not(inside))
    def _():
        last_all(16).wait_send()


def body(jacobian, energy):
    rows, params = jacobian.shape
    total = rows * lax.axis_size("samp") * lax.axis_size("par")
    tall = params // CHUNKS // LANES
    whole = (params // LANES, LANES)
    piece = (tall // 2, LANES)
    vmem = pl.BlockSpec(memory_space=pltpu.VMEM)
    dma = pltpu.SemaphoreType.DMA
    outs = pl.pallas_call(
        functools.partial(kernel, total),
        out_shape=pltpu.VMEM((2, *piece), f32),
        in_specs=[pl.BlockSpec(memory_space=pltpu.HBM)] * 2,
        out_specs=vmem,
        scratch_shapes=[
            pltpu.VMEM((energy.shape[0] // LANES, LANES), f32),
            pltpu.VMEM((rows, params), bf16),
            pltpu.VMEM((params, rows), bf16),
            pltpu.VMEM((tall, LANES), f32),
            pltpu.VMEM((2, CHUNKS, 2, *piece), bf16),
            pltpu.VMEM((2, CHUNKS, 8, *piece), bf16),
            pltpu.VMEM((2, CHUNKS, 16, *piece), bf16),
            pltpu.VMEM((16, *piece), bf16),
            pltpu.VMEM((CHUNKS, *piece), bf16),
            pltpu.VMEM((16, *piece), bf16),
            pltpu.VMEM((8, 1, LANES), f32),
            pltpu.VMEM((16, 1, LANES), f32),
            pltpu.VMEM(whole, f32),
            pltpu.VMEM(whole, f32),
            pltpu.VMEM(whole, f32),
            pltpu.VMEM((2, *whole), f32),
            pltpu.VMEM((2, *piece), f32),
            pltpu.VMEM((8, params // CHUNKS // 2), f32),
            dma,
            dma((CHUNKS,)),
        ]
        + [dma((2, CHUNKS))] * 6
        + [dma, dma, dma, dma, dma((2,)), dma((2,))],
        compiler_params=pltpu.CompilerParams(
            collective_id=0, has_side_effects=True, vmem_limit_bytes=56 * 2**20
        ),
    )(energy.reshape(-1, LANES), jacobian)
    return outs[0].reshape(-1), outs[1].reshape(-1)


def solution(mesh):
    return jax.shard_map(
        body,
        mesh=mesh,
        in_specs=(P(("samp", "par"), None), P("samp")),
        out_specs=(P("par"), P("par")),
        check_vma=False,
    )
```

```python
import functools

import jax
import jax.numpy as jnp
from jax import lax
from jax.experimental import pallas as pl
from jax.experimental.pallas import tpu as pltpu
from jax.sharding import PartitionSpec as P

ITERS = 3
DAMPING = 0.05
LANES = 128
CHUNKS = 4
MESH = pl.DeviceIdType.MESH
f32, bf16 = jnp.float32, jnp.bfloat16


def coordinates():
    samp, par = lax.axis_index("samp"), lax.axis_index("par")
    x = (samp // 8) * 2 + par // 4
    return x, par % 4, (samp // 2) % 4, samp % 2


def device(x, y, z, c):
    return ((x // 2) * 8 + z * 2 + c, (x % 2) * 4 + y)


def hops(*steps):
    return -sum(min(s, 4 - s) for s in steps)


def kernel(
    total,
    energy_hbm, jac_hbm, outs,
    energy, jac, jac_t, part, column_out, column, plane, cross, last_out, last, scalar_column, scalar_plane,
    update, residual, direction, image, narrow,
    energy_sem, load_sem, column_send, column_recv, plane_send, plane_recv, core_send, core_recv,
    cross_send, cross_recv, last_send, last_recv, scalar_send, scalar_recv,
):
    rows, params = jac.shape
    width = params // CHUNKS
    tall = width // LANES
    half = tall // 2
    x, y, z, c = coordinates()
    me = x * 4 + y
    own = c * 4 + z
    sibling = device(x, y, z, 1 - c)
    plane_peers = [
        device((x + a) % 4, (y + b) % 4, z, c)
        for a, b in sorted(((a, b) for a in range(4) for b in range(4) if a or b), key=lambda s: hops(*s))
    ]
    column_peers = [
        ((c + e) % 2, device(x, y, (z + d) % 4, (c + e) % 2))
        for d, e in sorted(((d, e) for d in range(4) for e in range(2) if d or e), key=lambda s: hops(s[0]))
    ]
    scale = 1.0 / total

    def load(i):
        columns = pl.ds(i * width, width)
        return pltpu.make_async_copy(jac_hbm.at[:, columns], jac.at[:, columns], load_sem.at[i])

    load_energy = pltpu.make_async_copy(energy_hbm, energy, energy_sem)
    load_energy.start()
    for i in range(2):
        load(i).start()

    barrier = pltpu.get_barrier_semaphore()
    others = [
        device((x + a) % 4, (y + b) % 4, z, 1 - c)
        for a, b in sorted(((a, b) for a in range(4) for b in range(4) if a or b), key=lambda s: hops(*s))
    ]
    greeted = plane_peers + others + [peer for _, peer in column_peers]
    for peer in greeted:
        pl.semaphore_signal(barrier, inc=1, device_id=peer, device_id_type=MESH)
    pl.semaphore_wait(barrier, len(greeted))

    def copy_to(peer, source, target, send, recv):
        return pltpu.make_async_remote_copy(
            source, target, send, recv, device_id=peer, device_id_type=MESH
        )

    def column_copy(p, k, core, peer):
        return copy_to(
            peer, column_out.at[p, k, core], column.at[p, k, own], column_send.at[p, k], column_recv.at[p, k]
        )

    def column_all(p, k):
        some = column.at[p, k, pl.ds(0, 7)]
        return copy_to(sibling, some, some, column_send.at[p, k], column_recv.at[p, k])

    def plane_copy(p, k, slot, peer):
        piece = plane.at[p, k, slot]
        return copy_to(peer, piece, piece, plane_send.at[p, k], plane_recv.at[p, k])

    def plane_all(p, k):
        return plane_copy(p, k, pl.ds(0, 15), sibling)

    def core_copy(p, k):
        piece = image.at[p, pl.ds(k * tall + c * half, half)]
        return copy_to(sibling, piece, piece, core_send.at[p, k], core_recv.at[p, k])

    def cross_copy(slot, source, peer):
        return copy_to(peer, source, cross.at[slot], cross_send, cross_recv)

    def each(step):
        lax.fori_loop(0, CHUNKS, lambda k, _: (step(k), 0)[1], 0)

    def multiply(k, h, count, vector):
        columns = pl.ds(k * width + h * width // 2, count * width // 2)
        product = jnp.dot(vector, jac[:, columns], preferred_element_type=f32)
        for i in range(count * half):
            part[h * half + i : h * half + i + 1] = product[:1, i * LANES : (i + 1) * LANES]

    def transpose(first, count):
        piece = 512

        def one(i, _):
            columns = pl.ds(pl.multiple_of(first + i * piece, piece), piece)
            jac_t[columns, :] = jac[:, columns].T
            return 0

        lax.fori_loop(0, count // piece, one, 0)

    def send_columns(p, row, first, between=None):
        vector = jnp.broadcast_to(row, (8, rows)).astype(bf16)
        for k in range(CHUNKS):
            if first:
                load(k).wait()
                if k + 2 < CHUNKS:
                    load(k + 2).start()
            multiply(k, 0, 2, vector)
            column_out[p, k, 0] = part[:half].astype(bf16)
            column_out[p, k, 1] = part[half:].astype(bf16)
            column[p, k, own] = column_out[p, k, c]
            for core, peer in column_peers:
                column_copy(p, k, core, peer).start()
            if between is not None and k == 0:
                between()

    def column_sum(p, k):
        column_all(p, k).wait_recv()
        return jnp.sum(column[p, k].astype(f32), axis=0).astype(bf16)

    def send_plane(p, k):
        plane[p, k, me] = column_sum(p, k)
        for peer in plane_peers:
            plane_copy(p, k, me, peer).start()

    def forward(p, k, h, transposed=True):
        value = image[p, pl.ds(k * tall + h * half, half)]
        high = value.astype(bf16).astype(f32)
        low = value - high
        for i in range(half):
            columns = slice(i * LANES, (i + 1) * LANES)
            narrow[0:1, columns] = high[i : i + 1]
            narrow[1:2, columns] = low[i : i + 1]
        depth = width // 2
        base = pl.multiple_of(k * width + h * depth, depth)
        terms = narrow[...].astype(bf16)
        if transposed:
            out = jnp.dot(terms, jac_t[pl.ds(base, depth), :], preferred_element_type=f32)
        else:
            out = lax.dot_general(
                terms, jac[:, pl.ds(base, depth)], (((1,), (1,)), ((), ())), preferred_element_type=f32
            )
        return out[0:1] + out[1:2]

    def mine(p, k, inner, exchange=True, transposed=True):
        plane_all(p, k).wait_recv()
        value = jnp.sum(plane[p, k].astype(f32), axis=0)
        image[p, pl.ds(k * tall + c * half, half)] = value * scale
        if exchange:
            core_copy(p, k).start()
        return inner + forward(p, k, c, transposed)

    def theirs(p, k, inner, transposed=True):
        core_copy(p, k).wait_recv()
        return inner + forward(p, k, 1 - c, transposed)

    def gather(p):
        inner = jnp.zeros((1, rows), f32)
        lag = 1
        for k in range(CHUNKS + lag):
            if k < CHUNKS:
                inner = mine(p, k, inner)
            if k >= lag:
                inner = theirs(p, k - lag, inner)
        return inner

    def gather_first(p):
        k = CHUNKS - 1
        inner = mine(p, 0, jnp.zeros((1, rows), f32), True, False)
        inner = mine(p, 1, inner, True, False)
        inner = theirs(p, 0, inner, False)
        inner = mine(p, 2, inner)
        inner = theirs(p, 1, inner, False)
        inner = mine(p, k, inner, False)
        inner = theirs(p, k - 1, inner)
        everything = pl.ds(0, 16)
        cross_copy(everything, cross.at[everything], sibling).wait()
        value = jnp.sum(cross[...].astype(f32), axis=0)
        image[p, pl.ds(k * tall + (1 - c) * half, half)] = value * scale
        return inner + forward(p, k, 1 - c)

    def drain(p, whole):
        def chunk(k):
            column_all(p, k).wait_send()
            plane_all(p, k).wait_send()

            @pl.when(jnp.logical_or(k < CHUNKS - 1, whole))
            def _():
                core_copy(p, k).wait_send()

        each(chunk)

    def dot(a, b):
        return jnp.sum(a * b, keepdims=True)

    narrow[...] = jnp.zeros(narrow.shape, f32)
    load_energy.wait()
    start = lax.axis_index("par") * (rows // LANES)
    deviation = jnp.concatenate(
        [energy[pl.ds(start + i, 1), :] for i in range(rows // LANES)], axis=1
    )
    update[...] = jnp.zeros(update.shape, f32)
    direction[...] = jnp.zeros(direction.shape, f32)
    send_columns(0, deviation, True)

    piece = width // 2
    send_plane(0, 0)
    transpose(2 * width + 0 * piece, piece)
    send_plane(0, 1)
    transpose(2 * width + 1 * piece, piece)
    send_plane(0, 2)
    transpose(2 * width + 2 * piece, piece)
    send_plane(0, 3)
    for peer in others + [sibling]:
        cross_copy(me, plane.at[0, 3, me], peer).start()
    transpose(2 * width + 3 * piece, piece)
    inner = gather_first(0)
    force = image[0]
    residual[...] = force
    norm = dot(force, force)

    def settle(p, alpha, beta, whole):
        update[...] = update[...] + alpha * direction[...]
        direction[...] = residual[...] + beta * direction[...]
        drain(p, whole)

    def step(it, carry):
        norm, alpha, beta, left, along = carry
        p = (it + 1) % 2
        send_columns(p, along, False)
        settle(1 - p, alpha, beta, it > 0)

        @pl.when(it == 0)
        def _():
            transpose(0, width)

        for k in range(CHUNKS):
            send_plane(p, k)

        @pl.when(it == 0)
        def _():
            transpose(width, width)

        inner = gather(p) + DAMPING * along
        applied = image[p] + DAMPING * direction[...]
        alpha = norm / dot(direction[...], applied)
        rest = residual[...] - alpha * applied
        residual[...] = rest
        new = dot(rest, rest)
        beta = new / norm
        left = left - alpha * inner
        return new, alpha, beta, left, left + beta * along

    zero = jnp.zeros((1, 1), f32)
    norm, alpha, beta, left, along = lax.fori_loop(0, ITERS - 1, step, (norm, zero, zero, inner, inner))

    p = ITERS % 2

    def scalar_copy(buffer, slot, stage, peer):
        piece = buffer.at[slot]
        return copy_to(peer, piece, piece, scalar_send.at[stage], scalar_recv.at[stage])

    def send_squares():
        squares = dot(along.astype(bf16).astype(f32), along)
        scalar_column[own] = jnp.broadcast_to(squares, (1, LANES))
        for _, peer in column_peers:
            scalar_copy(scalar_column, own, 0, peer).start()

    send_columns(p, along, False, send_squares)
    settle(1 - p, alpha, beta, True)
    scalar_copy(scalar_column, pl.ds(0, 7), 0, sibling).wait()
    scalar_plane[me] = jnp.sum(scalar_column[...], axis=0)
    for peer in plane_peers:
        scalar_copy(scalar_plane, me, 1, peer).start()

    def last_copy(source, slot, peer):
        return copy_to(peer, source, last.at[slot], last_send, last_recv)

    for k in range(CHUNKS):
        last_out[k] = column_sum(p, k)
        to_y = 2 * (k % 2) + c
        for to_x in (k // 2, k // 2 + 2):
            last_copy(last_out.at[k], me, device(to_x, to_y, z, 1 - c)).start()
            local = jnp.logical_and(x == to_x, y == to_y)

            @pl.when(jnp.logical_not(local))
            def _():
                last_copy(last_out.at[k], me, device(to_x, to_y, z, c)).start()

            @pl.when(local)
            def _():
                last[me] = last_out[k]

    scalar_copy(scalar_plane, pl.ds(0, 15), 1, sibling).wait()
    squares = jnp.sum(scalar_plane[...], axis=0)[:, :1] * scale
    alpha = norm / (squares + DAMPING * dot(direction[...], direction[...]))

    def last_all(count):
        return last_copy(last.at[pl.ds(0, count)], pl.ds(0, count), sibling)

    inside = y % 2 == c

    @pl.when(inside)
    def _():
        last_all(15).wait_recv()

    @pl.when(jnp.logical_not(inside))
    def _():
        last_all(16).wait_recv()

    value = jnp.sum(last[...].astype(f32), axis=0) * scale
    mine = pl.ds(lax.axis_index("par") * half, half)
    outs[0] = update[mine] + alpha * direction[mine]
    outs[1] = residual[mine] - alpha * (value + DAMPING * direction[mine])

    each(lambda k: column_all(p, k).wait_send())

    @pl.when(inside)
    def _():
        last_all(15).wait_send()

    @pl.when(jnp.logical_not(inside))
    def _():
        last_all(16).wait_send()


def body(jacobian, energy):
    rows, params = jacobian.shape
    total = rows * lax.axis_size("samp") * lax.axis_size("par")
    tall = params // CHUNKS // LANES
    whole = (params // LANES, LANES)
    piece = (tall // 2, LANES)
    vmem = pl.BlockSpec(memory_space=pltpu.VMEM)
    dma = pltpu.SemaphoreType.DMA
    outs = pl.pallas_call(
        functools.partial(kernel, total),
        out_shape=pltpu.VMEM((2, *piece), f32),
        in_specs=[pl.BlockSpec(memory_space=pltpu.HBM)] * 2,
        out_specs=vmem,
        scratch_shapes=[
            pltpu.VMEM((energy.shape[0] // LANES, LANES), f32),
            pltpu.VMEM((rows, params), bf16),
            pltpu.VMEM((params, rows), bf16),
            pltpu.VMEM((tall, LANES), f32),
            pltpu.VMEM((2, CHUNKS, 2, *piece), bf16),
            pltpu.VMEM((2, CHUNKS, 8, *piece), bf16),
            pltpu.VMEM((2, CHUNKS, 16, *piece), bf16),
            pltpu.VMEM((16, *piece), bf16),
            pltpu.VMEM((CHUNKS, *piece), bf16),
            pltpu.VMEM((16, *piece), bf16),
            pltpu.VMEM((8, 1, LANES), f32),
            pltpu.VMEM((16, 1, LANES), f32),
            pltpu.VMEM(whole, f32),
            pltpu.VMEM(whole, f32),
            pltpu.VMEM(whole, f32),
            pltpu.VMEM((2, *whole), f32),
            pltpu.VMEM((8, params // CHUNKS // 2), f32),
            dma,
            dma((CHUNKS,)),
        ]
        + [dma((2, CHUNKS))] * 6
        + [dma, dma, dma, dma, dma((2,)), dma((2,))],
        compiler_params=pltpu.CompilerParams(
            collective_id=0, has_side_effects=True, vmem_limit_bytes=56 * 2**20
        ),
    )(energy.reshape(-1, LANES), jacobian)
    return outs[0].reshape(-1), outs[1].reshape(-1)


def solution(mesh):
    return jax.shard_map(
        body,
        mesh=mesh,
        in_specs=(P(("samp", "par"), None), P("samp")),
        out_specs=(P("par"), P("par")),
        check_vma=False,
    )
```
